32 devices in a mesh: section: 4 (over z), seq: 4 (over y, core), dp: 2 (over x).
Axes of the slice: x: 2, y: 2, z: 4, core: 2. Of those that a mesh axis runs over, the one named last changes fastest.
Arguments:
- layer_input: bfloat16 [4, 2, 512, 2048], P('section', 'dp', 'seq'), may hold values from -6 to 6
- tangent_input: bfloat16 [4, 2, 512, 2048], P('section', 'dp', 'seq'), may hold values from -6 to 6
- cotangent_input: bfloat16 [4, 2, 512, 2048], P('section', 'dp', 'seq'), may hold values from -6 to 6
- saved_normed: bfloat16 [4, 2, 512, 2048], P('section', 'dp'), may hold values from -6 to 6
- saved_inv_rms: float32 [4, 2, 512], P('section', 'dp', 'seq'), may hold values from 0.5 to 2
- saved_projections: bfloat16 [4, 2, 512, 4, 384], P('section', 'dp', None, 'seq'), may hold values from -6 to 6
- time_index: int32 [4, 2, 2], P('section', 'dp'), may hold values from 0 to 999
- input_weight: bfloat16 [4, 2048, 4, 384], P('section', None, 'seq'), may hold values from -3 to 3
- output_weight: bfloat16 [4, 4, 128, 2048], P('section'), may hold values from -0.25 to 0.25
- norm_gain: float32 [4, 2048], P('section'), may hold values from 0.5 to 1.5
- time_scale: float32 [4, 2048], P('section'), may hold values from -0.3 to 0.3
Outputs:
- next_input: bfloat16 [4, 2, 512, 2048], P('section', 'dp', 'seq')
- next_tangent: bfloat16 [4, 2, 512, 2048], P('section', 'dp', 'seq')
- prev_cotangent: bfloat16 [4, 2, 512, 2048], P('section', 'dp', 'seq')
- input_weight_gradient: float32 [4, 2048, 4, 384], P('section', 'dp', 'seq')
- output_weight_gradient: float32 [4, 4, 128, 2048], P('section', 'seq', None, 'dp')
- modulation_gradient: float32 [4, 2, 2048], P('section')
The draws below stay inside these ranges and needn't reach their ends.
Inputs may be any that keep to these rules, and one draw needn't show every extreme that they name: `time_index`: index 0 of the last dimension is the forward micro-batch's, 1 the backward micro-batch's.
All inputs are finite; a program needn't handle non-finite values.
Results may differ from the reference program's by a relative error of at most 0.014.
Values may be sent and summed in bfloat16 or wider, within the bound.
A program may use at most 128 MiB of HBM per device.

```python
import math
import jax
import jax.numpy as jnp
from jax import lax

D = 2048
HD = 128
TSTEPS = 1000
TOKENS = 512
HEADS = 4
N_SECTION = 4
N_DP = 2


def paired_rows(key, salt_value):
    drawn = jax.random.truncated_normal(jax.random.fold_in(key, salt_value), -6.0, 6.0, (N_SECTION * N_DP, TOKENS, D), jnp.float32)
    return drawn.reshape(N_SECTION, N_DP, TOKENS, D).astype(jnp.bfloat16)


def draw_layer_input(key, part):
    return paired_rows(key, 101)


def draw_tangent_input(key, part):
    return paired_rows(key, 202)


def draw_saved_projections(key, part):
    drawn = jax.random.truncated_normal(jax.random.fold_in(key, 31), -6.0, 6.0, (N_SECTION, N_DP, TOKENS, HEADS, 3 * HD), jnp.float32)
    return drawn.astype(jnp.bfloat16)


def draw_input_weight(key, part):
    drawn = jax.random.truncated_normal(jax.random.fold_in(key, 53), -4.0, 4.0, (N_SECTION, D, HEADS, 3 * HD), jnp.float32) * D ** (-0.5)
    return drawn.astype(jnp.bfloat16)


def plant(array, rng, low, largest):
    longest = array.shape.index(max(array.shape))
    spots = []
    for shift in (0, 1):
        where = [jax.random.randint(jax.random.fold_in(rng, axis), (), 0, length) for axis, length in enumerate(array.shape)]
        where[longest] = (where[longest] + shift) % array.shape[longest]
        spots.append(tuple(where))
    return array.at[spots[0]].set(low).at[spots[1]].set(largest)


def block_scale(key, dims, pieces, smallest, top_value):
    def one(position, blocks):
        steps = jax.random.uniform(jax.random.fold_in(jax.random.fold_in(key, 6), position), (blocks,), jnp.float32, smallest / len(pieces), top_value / len(pieces))
        return jnp.repeat(jnp.exp(steps), dims[position] // blocks).reshape((-1,) + (1,) * (len(dims) - position - 1))

    factor_of = one(*pieces[0])
    for cut in pieces[1:]:
        factor_of = factor_of * one(*cut)
    return factor_of


def scatter_about(rng, shape, scale, reach, pieces=(), kind=jnp.bfloat16):
    values = scale * jax.random.normal(rng, shape, jnp.float32)
    if pieces:
        values = values * block_scale(rng, shape, pieces, -0.22, 0.18)
    return jnp.clip(values, -reach, reach).astype(kind)


def setup_inputs(seed: int = 0) -> dict:
    seeds = jax.random.split(jax.random.key(seed), 12)
    return {
        "layer_input": draw_layer_input(jax.random.fold_in(seeds[11], 71), 0),
        "tangent_input": draw_tangent_input(jax.random.fold_in(seeds[11], 71), 0),
        "cotangent_input": scatter_about(seeds[2], (N_SECTION, N_DP, TOKENS, D), 1.0, 6.0, ((0, 4), (1, 2), (2, 4))),
        "saved_normed": scatter_about(seeds[3], (N_SECTION, N_DP, TOKENS, D), 1.0, 6.0, ((0, 4), (1, 2))),
        "saved_inv_rms": jnp.clip(jnp.exp(math.log(2.0) - 1.3862944 * jax.random.uniform(seeds[4], (N_SECTION, N_DP, TOKENS), jnp.float32) ** block_scale(seeds[4], (N_SECTION, N_DP, TOKENS), ((0, 4), (1, 2), (2, 4)), -0.2, 0.2)), 0.5, 2.0),
        "saved_projections": draw_saved_projections(jax.random.fold_in(seeds[11], 71), 0),
        "time_index": plant(jax.random.randint(seeds[6], (N_SECTION, N_DP, 2), 0, TSTEPS), jax.random.fold_in(seeds[6], 1), 0, TSTEPS - 1).astype(jnp.int32),
        "input_weight": draw_input_weight(jax.random.fold_in(seeds[11], 71), 0),
        "output_weight": scatter_about(seeds[8], (N_SECTION, HEADS, HD, D), (HEADS * HD) ** -0.5, 0.25, ((0, 4),)),
        "norm_gain": jnp.clip(1.0 + 0.1 * jax.random.normal(seeds[9], (N_SECTION, D), jnp.float32), 0.5, 1.5),
        "time_scale": jnp.clip(jax.random.uniform(seeds[10], (N_SECTION, D), jnp.float32, -0.3, 0.3) * block_scale(seeds[10], (N_SECTION, D), ((0, 4),), -0.4, 0.0), -0.3, 0.3),
    }


EPS = 1e-06

def timesteps(indices):
    return math.pi / 2 * (indices.astype(jnp.float32) + 0.5) / TSTEPS

def attend_tangent(queries, keys, values, tan_queries, tan_keys, tan_values):
    rows = queries.shape[0]
    block_rows = min(512, rows)
    scale = 1.0 / math.sqrt(queries.shape[1])

    def one_block(inputs):
        query_block, tangent_block = inputs
        scores = jnp.einsum('qd,kd->qk', query_block, keys, preferred_element_type=jnp.float32) * scale
        probs = jax.nn.softmax(scores, axis=-1)
        tan_scores = (jnp.einsum('qd,kd->qk', tangent_block, keys, preferred_element_type=jnp.float32) + jnp.einsum('qd,kd->qk', query_block, tan_keys, preferred_element_type=jnp.float32)) * scale
        tan_probs = probs * (tan_scores - lax.optimization_barrier(jnp.sum(probs * tan_scores, -1, keepdims=True)))
        probs_low = probs.astype(jnp.bfloat16)
        tan_low = tan_probs.astype(jnp.bfloat16)
        attended = jnp.dot(probs_low, values, preferred_element_type=jnp.float32)
        tan_attended = jnp.dot(tan_low, values, preferred_element_type=jnp.float32) + jnp.dot(probs_low, tan_values, preferred_element_type=jnp.float32)
        return (attended.astype(jnp.bfloat16), tan_attended.astype(jnp.bfloat16))
    shaped = (queries.reshape(rows // block_rows, block_rows, -1), tan_queries.reshape(rows // block_rows, block_rows, -1))
    attended, tan_attended = lax.map(one_block, shaped)
    return (attended.reshape(rows, -1), tan_attended.reshape(rows, -1))

def attend_backward(queries, keys, values, grad_attended):
    rows, head_size = queries.shape
    block_rows = min(512, rows)
    scale = 1.0 / math.sqrt(head_size)

    def one_block(carry, inputs):
        grad_keys, grad_values = carry
        query_block, grad_block = inputs
        scores = jnp.einsum('qd,kd->qk', query_block, keys, preferred_element_type=jnp.float32) * scale
        probs = jax.nn.softmax(scores, axis=-1)
        probs_low = probs.astype(jnp.bfloat16)
        attended = jnp.dot(probs_low, values, preferred_element_type=jnp.float32).astype(jnp.bfloat16)
        grad_values = grad_values + jnp.einsum('qk,qd->kd', probs_low, grad_block, preferred_element_type=jnp.float32)
        grad_probs = jnp.einsum('qd,kd->qk', grad_block, values, preferred_element_type=jnp.float32)
        grad_scores = probs * (grad_probs - lax.optimization_barrier(jnp.sum(probs * grad_probs, -1, keepdims=True))) * scale
        grad_low = grad_scores.astype(jnp.bfloat16)
        grad_queries = jnp.dot(grad_low, keys, preferred_element_type=jnp.float32)
        grad_keys = grad_keys + jnp.einsum('qk,qd->kd', grad_low, query_block, preferred_element_type=jnp.float32)
        return ((grad_keys, grad_values), (grad_queries, attended))
    zeros = jnp.zeros((rows, head_size), jnp.float32)
    shaped = (queries.reshape(rows // block_rows, block_rows, head_size), grad_attended.reshape(rows // block_rows, block_rows, head_size))
    (grad_keys, grad_values), (grad_queries, attended) = lax.scan(one_block, (zeros, zeros), shaped)
    return (grad_queries.reshape(rows, head_size), grad_keys, grad_values, attended.reshape(rows, head_size))

def reference(layer_input, tangent_input, cotangent_input, saved_normed, saved_inv_rms, saved_projections, time_index, input_weight, output_weight, norm_gain, time_scale):
    width = input_weight.shape[1]
    heads = input_weight.shape[2]
    head_size = input_weight.shape[3] // 3
    total = layer_input.shape[2]
    outputs_fwd = []
    tangents_fwd = []
    cotangents = []
    qkv_grads = []
    out_grads = []
    mod_grads = []
    for section_num in range(N_SECTION):
        weight_heads = input_weight[section_num]
        output_flat = output_weight[section_num].reshape(heads * head_size, width)
        section_outputs = []
        section_tangents = []
        section_cots = []
        qkv_sum = jnp.zeros((heads, width, 3 * head_size), jnp.float32)
        out_sum = jnp.zeros((heads, head_size, width), jnp.float32)
        mod_sum = jnp.zeros((2, width), jnp.float32)
        for clip_num in range(N_DP):
            times = timesteps(time_index[section_num, clip_num])
            hidden = layer_input[section_num, clip_num].astype(jnp.float32)
            tangent = tangent_input[section_num, clip_num].astype(jnp.float32)
            inverse = lax.rsqrt(lax.optimization_barrier(jnp.mean(hidden * hidden, -1, keepdims=True)) + EPS)
            normal = hidden * inverse
            tan_inverse = -inverse ** 3 * lax.optimization_barrier(jnp.mean(hidden * tangent, -1, keepdims=True))
            tan_normal = tangent * inverse + hidden * tan_inverse
            modulated = norm_gain[section_num] + jnp.sin(times[0]) * time_scale[section_num]
            tan_modulated = jnp.cos(times[0]) * time_scale[section_num]
            normed = (normal * modulated).astype(jnp.bfloat16)
            tan_normed = (tan_normal * modulated + normal * tan_modulated).astype(jnp.bfloat16)
            stacked = jnp.stack([normed, tan_normed])
            projected = jnp.einsum('srd,dc->src', stacked, weight_heads.reshape(width, heads * 3 * head_size), preferred_element_type=jnp.float32).astype(jnp.bfloat16)
            projected = projected.reshape(2, total, heads, 3 * head_size).transpose(2, 0, 1, 3)

            def head_forward(group_in):
                return attend_tangent(group_in[0, :, :head_size], group_in[0, :, head_size:2 * head_size], group_in[0, :, 2 * head_size:], group_in[1, :, :head_size], group_in[1, :, head_size:2 * head_size], group_in[1, :, 2 * head_size:])
            attended, tan_attended = lax.map(head_forward, projected)
            attended = attended.transpose(1, 0, 2).reshape(total, heads * head_size)
            tan_attended = tan_attended.transpose(1, 0, 2).reshape(total, heads * head_size)
            section_outputs.append((hidden + jnp.dot(attended, output_flat, preferred_element_type=jnp.float32)).astype(jnp.bfloat16))
            section_tangents.append((tangent + jnp.dot(tan_attended, output_flat, preferred_element_type=jnp.float32)).astype(jnp.bfloat16))
            cot_rows = cotangent_input[section_num, clip_num]
            normed_all = saved_normed[section_num, clip_num]

            def head_backward(carry, inputs):
                saved_head, out_head, weight_head = inputs
                grad_out = jnp.einsum('td,hd->th', cot_rows, out_head, preferred_element_type=jnp.float32).astype(jnp.bfloat16)
                grad_q, grad_k, grad_v, attended_b = attend_backward(saved_head[:, :head_size], saved_head[:, head_size:2 * head_size], saved_head[:, 2 * head_size:], grad_out)
                out_grad = jnp.einsum('th,td->hd', attended_b, cot_rows, preferred_element_type=jnp.float32)
                grad_proj = jnp.concatenate([grad_q, grad_k, grad_v], -1).astype(jnp.bfloat16)
                qkv_grad = jnp.einsum('td,tc->dc', normed_all, grad_proj, preferred_element_type=jnp.float32)
                term = jnp.einsum('tc,dc->td', grad_proj, weight_head, preferred_element_type=jnp.float32).astype(jnp.bfloat16)
                term = lax.optimization_barrier(term)
                return (carry + term.astype(jnp.float32), (qkv_grad, out_grad))
            start = jnp.zeros((total, width), jnp.float32)
            grad_normed, (qkv_part, out_part) = lax.scan(head_backward, start, (saved_projections[section_num, clip_num].transpose(1, 0, 2), output_weight[section_num], weight_heads.transpose(1, 0, 2)))
            modulated_b = norm_gain[section_num] + jnp.sin(times[1]) * time_scale[section_num]
            normal_b = normed_all.astype(jnp.float32) / modulated_b
            weighted = grad_normed * modulated_b
            grad_hidden = saved_inv_rms[section_num, clip_num][:, None] * (weighted - normal_b * lax.optimization_barrier(jnp.mean(normal_b * weighted, -1, keepdims=True)))
            section_cots.append((cot_rows.astype(jnp.float32) + grad_hidden).astype(jnp.bfloat16))
            gain_part = lax.optimization_barrier(jnp.sum(grad_normed * normal_b, 0))
            mod_sum = mod_sum + jnp.stack([gain_part, jnp.sin(times[1]) * gain_part])
            qkv_sum = qkv_sum + qkv_part
            out_sum = out_sum + out_part
        outputs_fwd.append(jnp.stack(section_outputs))
        tangents_fwd.append(jnp.stack(section_tangents))
        cotangents.append(jnp.stack(section_cots))
        qkv_grads.append(qkv_sum.transpose(1, 0, 2))
        out_grads.append(out_sum)
        mod_grads.append(mod_sum)
    next_input = jnp.roll(jnp.stack(outputs_fwd), 1, axis=0)
    next_tangent = jnp.roll(jnp.stack(tangents_fwd), 1, axis=0)
    prev_cotangent = jnp.roll(jnp.stack(cotangents), -1, axis=0)
    return (next_input, next_tangent, prev_cotangent, jnp.stack(qkv_grads), jnp.stack(out_grads), jnp.stack(mod_grads))
```

```python
import math

import jax
import jax.numpy as jnp
from jax import lax
from jax.sharding import PartitionSpec as P

TSTEPS = 1000


EPS = 1e-06


def passed_along(value, axis, steps):
    count = lax.axis_size(axis)
    pairs = [(source, (source + steps) % count) for source in range(count)]
    return lax.ppermute(value, axis, pairs)


def timesteps(indices):
    return math.pi / 2 * (indices.astype(jnp.float32) + 0.5) / TSTEPS


def attend_tangent(queries, keys, values, tan_queries, tan_keys, tan_values):
    rows = queries.shape[0]
    block_rows = min(512, rows)
    scale = 1.0 / math.sqrt(queries.shape[1])

    def one_block(inputs):
        query_block, tangent_block = inputs
        scores = (
            jnp.einsum("qd,kd->qk", query_block, keys, preferred_element_type=jnp.float32) * scale
        )
        probs = jax.nn.softmax(scores, axis=-1)
        tan_scores = (
            jnp.einsum("qd,kd->qk", tangent_block, keys, preferred_element_type=jnp.float32)
            + jnp.einsum("qd,kd->qk", query_block, tan_keys, preferred_element_type=jnp.float32)
        ) * scale
        tan_probs = probs * (tan_scores - jnp.sum(probs * tan_scores, -1, keepdims=True))
        probs_low = probs.astype(jnp.bfloat16)
        tan_low = tan_probs.astype(jnp.bfloat16)
        attended = jnp.dot(probs_low, values, preferred_element_type=jnp.float32)
        tan_attended = jnp.dot(tan_low, values, preferred_element_type=jnp.float32) + jnp.dot(
            probs_low, tan_values, preferred_element_type=jnp.float32
        )
        return (attended.astype(jnp.bfloat16), tan_attended.astype(jnp.bfloat16))

    shaped = (
        queries.reshape(rows // block_rows, block_rows, -1),
        tan_queries.reshape(rows // block_rows, block_rows, -1),
    )
    attended, tan_attended = lax.map(one_block, shaped)
    return (attended.reshape(rows, -1), tan_attended.reshape(rows, -1))


def attend_backward(queries, keys, values, grad_attended):
    rows, head_size = queries.shape
    block_rows = min(512, rows)
    scale = 1.0 / math.sqrt(head_size)

    def one_block(carry, inputs):
        grad_keys, grad_values = carry
        query_block, grad_block = inputs
        scores = (
            jnp.einsum("qd,kd->qk", query_block, keys, preferred_element_type=jnp.float32) * scale
        )
        probs = jax.nn.softmax(scores, axis=-1)
        probs_low = probs.astype(jnp.bfloat16)
        attended = jnp.dot(probs_low, values, preferred_element_type=jnp.float32).astype(
            jnp.bfloat16
        )
        grad_values = grad_values + jnp.einsum(
            "qk,qd->kd", probs_low, grad_block, preferred_element_type=jnp.float32
        )
        grad_probs = jnp.einsum("qd,kd->qk", grad_block, values, preferred_element_type=jnp.float32)
        grad_scores = probs * (grad_probs - jnp.sum(probs * grad_probs, -1, keepdims=True)) * scale
        grad_low = grad_scores.astype(jnp.bfloat16)
        grad_queries = jnp.dot(grad_low, keys, preferred_element_type=jnp.float32)
        grad_keys = grad_keys + jnp.einsum(
            "qk,qd->kd", grad_low, query_block, preferred_element_type=jnp.float32
        )
        return ((grad_keys, grad_values), (grad_queries, attended))

    zeros = jnp.zeros((rows, head_size), jnp.float32)
    shaped = (
        queries.reshape(rows // block_rows, block_rows, head_size),
        grad_attended.reshape(rows // block_rows, block_rows, head_size),
    )
    (grad_keys, grad_values), (grad_queries, attended) = lax.scan(one_block, (zeros, zeros), shaped)
    return (
        grad_queries.reshape(rows, head_size),
        grad_keys,
        grad_values,
        attended.reshape(rows, head_size),
    )


def swapped(value, axis, mask):
    count = lax.axis_size(axis)
    return lax.ppermute(value, axis, [(source, source ^ mask) for source in range(count)])


def gathered(value):
    count = lax.axis_size("seq")
    pieces = {0: value}
    for mask in range(2, count, 2):
        pieces[mask] = swapped(value, "seq", mask)
    for mask in range(1, count, 2):
        pieces[mask] = swapped(pieces[mask ^ 1], "seq", 1)
    return [pieces[mask] for mask in range(count)]


def summed_to_owner(terms):
    count = len(terms)
    pairs = {}
    for mask in list(range(2, count, 2)) + [0]:
        other = swapped(terms[mask ^ 1], "seq", 1)
        pairs[mask] = terms[mask].astype(jnp.float32) + other.astype(jnp.float32)
    total = pairs[0]
    for mask in range(2, count, 2):
        total = total + swapped(pairs[mask].astype(jnp.bfloat16), "seq", mask).astype(jnp.float32)
    return total


def scattered_over_dp(value, axis):
    count = lax.axis_size("dp")
    me = lax.axis_index("dp")
    length = value.shape[axis] // count
    total = lax.dynamic_slice_in_dim(value, me * length, length, axis)
    for step in range(1, count):
        part = lax.dynamic_slice_in_dim(value, lax.rem(me + step, count) * length, length, axis)
        total = total + passed_along(part.astype(jnp.bfloat16), "dp", step).astype(jnp.float32)
    return total


def summed_everywhere(value):
    for axis in ("seq", "dp"):
        mask = 1
        while mask < lax.axis_size(axis):
            value = value + swapped(value, axis, mask)
            mask *= 2
    return value


def local(
    layer_input,
    tangent_input,
    cotangent_input,
    saved_normed,
    saved_inv_rms,
    saved_projections,
    time_index,
    input_weight,
    output_weight,
    norm_gain,
    time_scale,
):
    count = lax.axis_size("seq")
    me = lax.axis_index("seq")
    weight_heads = input_weight[0, :, 0, :]
    output_whole = output_weight[0]
    heads, head_size, width = output_whole.shape
    output_flat = output_whole.reshape(heads * head_size, width)
    output_head = lax.dynamic_index_in_dim(output_whole, me, 0, keepdims=False)
    gains = norm_gain[0]
    scales = time_scale[0]
    moments = timesteps(time_index[0, 0])
    cot_rows = cotangent_input[0, 0]
    normed_all = saved_normed[0, 0]
    inv_rows = saved_inv_rms[0, 0]
    saved_heads = saved_projections[0, 0, :, 0, :]
    rows = cot_rows.shape[0]
    owners = [jnp.bitwise_xor(me, mask) for mask in range(count)]

    cot_pieces = gathered(cot_rows)
    moment = moments[0]
    hidden = layer_input[0, 0].astype(jnp.float32)
    tangent = tangent_input[0, 0].astype(jnp.float32)
    inverse = lax.rsqrt(jnp.mean(hidden * hidden, -1, keepdims=True) + EPS)
    normal = hidden * inverse
    tan_inverse = -(inverse**3) * jnp.mean(hidden * tangent, -1, keepdims=True)
    tan_normal = tangent * inverse + hidden * tan_inverse
    modulated = gains + jnp.sin(moment) * scales
    tan_modulated = jnp.cos(moment) * scales
    normed = (normal * modulated).astype(jnp.bfloat16)
    tan_normed = (tan_normal * modulated + normal * tan_modulated).astype(jnp.bfloat16)
    normed_pieces = gathered(normed)
    tan_pieces = gathered(tan_normed)

    grad_out = jnp.zeros((rows * count, head_size), jnp.bfloat16)
    for mask in range(count):
        piece = jnp.einsum(
            "td,hd->th", cot_pieces[mask], output_head, preferred_element_type=jnp.float32
        ).astype(jnp.bfloat16)
        grad_out = lax.dynamic_update_slice_in_dim(grad_out, piece, owners[mask] * rows, 0)
    grad_q, grad_k, grad_v, attended_b = attend_backward(
        saved_heads[:, :head_size],
        saved_heads[:, head_size : 2 * head_size],
        saved_heads[:, 2 * head_size :],
        grad_out,
    )
    grad_proj = jnp.concatenate([grad_q, grad_k, grad_v], -1).astype(jnp.bfloat16)
    terms = {}
    for mask in reversed(range(count)):
        piece = lax.dynamic_slice_in_dim(grad_proj, owners[mask] * rows, rows, 0)
        terms[mask] = jnp.einsum(
            "tc,dc->td", piece, weight_heads, preferred_element_type=jnp.float32
        ).astype(jnp.bfloat16)
    grad_normed = summed_to_owner([terms[mask] for mask in range(count)])
    qkv_grad = jnp.einsum("td,tc->dc", normed_all, grad_proj, preferred_element_type=jnp.float32)
    out_grad = jnp.zeros((head_size, width), jnp.float32)
    for mask in range(count):
        piece = lax.dynamic_slice_in_dim(attended_b, owners[mask] * rows, rows, 0)
        out_grad = out_grad + jnp.einsum(
            "th,td->hd", piece, cot_pieces[mask], preferred_element_type=jnp.float32
        )
    qkv_total = scattered_over_dp(qkv_grad, 0)
    out_total = scattered_over_dp(out_grad, 1)

    def projected(pieces):
        return jnp.concatenate(
            [
                jnp.dot(piece, weight_heads, preferred_element_type=jnp.float32).astype(
                    jnp.bfloat16
                )
                for piece in pieces
            ]
        )

    proj = projected(normed_pieces)
    tan_proj = projected(tan_pieces)
    attended, tan_attended = attend_tangent(
        proj[:, :head_size],
        proj[:, head_size : 2 * head_size],
        proj[:, 2 * head_size :],
        tan_proj[:, :head_size],
        tan_proj[:, head_size : 2 * head_size],
        tan_proj[:, 2 * head_size :],
    )
    both = jnp.stack([attended, tan_attended])
    moved = jnp.zeros((2, rows, heads * head_size), jnp.bfloat16)
    for mask in range(count):
        piece = both[:, mask * rows : (mask + 1) * rows]
        if mask:
            piece = swapped(piece, "seq", mask)
        moved = lax.dynamic_update_slice_in_dim(moved, piece, owners[mask] * head_size, 2)
    result = hidden + jnp.dot(moved[0], output_flat, preferred_element_type=jnp.float32)
    next_input = passed_along(result.astype(jnp.bfloat16), "section", 1)
    result = tangent + jnp.dot(moved[1], output_flat, preferred_element_type=jnp.float32)
    next_tangent = passed_along(result.astype(jnp.bfloat16), "section", 1)

    moment = moments[1]
    own_normed = lax.dynamic_slice_in_dim(normed_all, me * rows, rows, 0)
    modulated = gains + jnp.sin(moment) * scales
    normal_b = own_normed.astype(jnp.float32) / modulated
    weighted = grad_normed * modulated
    grad_hidden = inv_rows[:, None] * (
        weighted - normal_b * jnp.mean(normal_b * weighted, -1, keepdims=True)
    )
    cotangent = (cot_rows.astype(jnp.float32) + grad_hidden).astype(jnp.bfloat16)
    cot_prev = passed_along(cotangent, "section", -1)
    gain_part = jnp.sum(grad_normed * normal_b, 0)
    norm_total = summed_everywhere(jnp.stack([gain_part, jnp.sin(moment) * gain_part]))
    return (
        next_input[None, None],
        next_tangent[None, None],
        cot_prev[None, None],
        qkv_total[None, :, None, :],
        out_total[None, None],
        norm_total[None],
    )


def solution(mesh):
    placed = (
        P("section", "dp", "seq", None),
        P("section", "dp", "seq", None),
        P("section", "dp", "seq", None),
        P("section", "dp", None, None),
        P("section", "dp", "seq"),
        P("section", "dp", None, "seq", None),
        P("section", "dp", None),
        P("section", None, "seq", None),
        P("section", None, None, None),
        P("section", None),
        P("section", None),
    )
    return jax.shard_map(
        local,
        mesh=mesh,
        in_specs=placed,
        out_specs=(
            P("section", "dp", "seq", None),
            P("section", "dp", "seq", None),
            P("section", "dp", "seq", None),
            P("section", "dp", "seq", None),
            P("section", "seq", None, "dp"),
            P("section", None, None),
        ),
        check_vma=False,
    )
```

```python
import math

import jax
import jax.numpy as jnp
from jax import lax
from jax.sharding import PartitionSpec as P

TSTEPS = 1000


EPS = 1e-06


def passed_along(value, axis, steps):
    count = lax.axis_size(axis)
    pairs = [(source, (source + steps) % count) for source in range(count)]
    return lax.ppermute(value, axis, pairs)


def timesteps(indices):
    return math.pi / 2 * (indices.astype(jnp.float32) + 0.5) / TSTEPS


def attend_tangent(queries, keys, values, tan_queries, tan_keys, tan_values):
    rows = queries.shape[0]
    block_rows = min(512, rows)
    scale = 1.0 / math.sqrt(queries.shape[1])

    def one_block(inputs):
        query_block, tangent_block = inputs
        scores = (
            jnp.einsum("qd,kd->qk", query_block, keys, preferred_element_type=jnp.float32) * scale
        )
        probs = jax.nn.softmax(scores, axis=-1)
        tan_scores = (
            jnp.einsum("qd,kd->qk", tangent_block, keys, preferred_element_type=jnp.float32)
            + jnp.einsum("qd,kd->qk", query_block, tan_keys, preferred_element_type=jnp.float32)
        ) * scale
        tan_probs = probs * (tan_scores - jnp.sum(probs * tan_scores, -1, keepdims=True))
        probs_low = probs.astype(jnp.bfloat16)
        tan_low = tan_probs.astype(jnp.bfloat16)
        attended = jnp.dot(probs_low, values, preferred_element_type=jnp.float32)
        tan_attended = jnp.dot(tan_low, values, preferred_element_type=jnp.float32) + jnp.dot(
            probs_low, tan_values, preferred_element_type=jnp.float32
        )
        return (attended.astype(jnp.bfloat16), tan_attended.astype(jnp.bfloat16))

    shaped = (
        queries.reshape(rows // block_rows, block_rows, -1),
        tan_queries.reshape(rows // block_rows, block_rows, -1),
    )
    attended, tan_attended = lax.map(one_block, shaped)
    return (attended.reshape(rows, -1), tan_attended.reshape(rows, -1))


def attend_backward(queries, keys, values, grad_attended):
    rows, head_size = queries.shape
    block_rows = min(512, rows)
    scale = 1.0 / math.sqrt(head_size)

    def one_block(carry, inputs):
        grad_keys, grad_values = carry
        query_block, grad_block = inputs
        scores = (
            jnp.einsum("qd,kd->qk", query_block, keys, preferred_element_type=jnp.float32) * scale
        )
        probs = jax.nn.softmax(scores, axis=-1)
        probs_low = probs.astype(jnp.bfloat16)
        attended = jnp.dot(probs_low, values, preferred_element_type=jnp.float32).astype(
            jnp.bfloat16
        )
        grad_values = grad_values + jnp.einsum(
            "qk,qd->kd", probs_low, grad_block, preferred_element_type=jnp.float32
        )
        grad_probs = jnp.einsum("qd,kd->qk", grad_block, values, preferred_element_type=jnp.float32)
        grad_scores = probs * (grad_probs - jnp.sum(probs * grad_probs, -1, keepdims=True)) * scale
        grad_low = grad_scores.astype(jnp.bfloat16)
        grad_queries = jnp.dot(grad_low, keys, preferred_element_type=jnp.float32)
        grad_keys = grad_keys + jnp.einsum(
            "qk,qd->kd", grad_low, query_block, preferred_element_type=jnp.float32
        )
        return ((grad_keys, grad_values), (grad_queries, attended))

    zeros = jnp.zeros((rows, head_size), jnp.float32)
    shaped = (
        queries.reshape(rows // block_rows, block_rows, head_size),
        grad_attended.reshape(rows // block_rows, block_rows, head_size),
    )
    (grad_keys, grad_values), (grad_queries, attended) = lax.scan(one_block, (zeros, zeros), shaped)
    return (
        grad_queries.reshape(rows, head_size),
        grad_keys,
        grad_values,
        attended.reshape(rows, head_size),
    )


def swapped(value, axis, mask):
    count = lax.axis_size(axis)
    return lax.ppermute(value, axis, [(source, source ^ mask) for source in range(count)])


def from_chips(value):
    return [swapped(value, "seq", mask) for mask in range(2, lax.axis_size("seq"), 2)]


def gathered(value, others):
    pieces = []
    for piece in [value] + others:
        pieces += [piece, swapped(piece, "seq", 1)]
    return pieces


def summed_to_owner(terms):
    count = len(terms)
    pairs = {}
    for mask in list(range(2, count, 2)) + [0]:
        other = swapped(terms[mask ^ 1], "seq", 1)
        pairs[mask] = terms[mask].astype(jnp.float32) + other.astype(jnp.float32)
    total = pairs[0]
    for mask in range(2, count, 2):
        total = total + swapped(pairs[mask].astype(jnp.bfloat16), "seq", mask).astype(jnp.float32)
    return total


def scattered_over_dp(value, axis):
    count = lax.axis_size("dp")
    me = lax.axis_index("dp")
    length = value.shape[axis] // count
    total = lax.dynamic_slice_in_dim(value, me * length, length, axis)
    for step in range(1, count):
        part = lax.dynamic_slice_in_dim(value, lax.rem(me + step, count) * length, length, axis)
        total = total + passed_along(part.astype(jnp.bfloat16), "dp", step).astype(jnp.float32)
    return total


def summed_everywhere(value):
    for axis in ("seq", "dp"):
        mask = 1
        while mask < lax.axis_size(axis):
            value = value + swapped(value, axis, mask)
            mask *= 2
    return value


def local(
    layer_input,
    tangent_input,
    cotangent_input,
    saved_normed,
    saved_inv_rms,
    saved_projections,
    time_index,
    input_weight,
    output_weight,
    norm_gain,
    time_scale,
):
    count = lax.axis_size("seq")
    me = lax.axis_index("seq")
    weight_heads = input_weight[0, :, 0, :]
    output_whole = output_weight[0]
    heads, head_size, width = output_whole.shape
    output_flat = output_whole.reshape(heads * head_size, width)
    output_head = lax.dynamic_index_in_dim(output_whole, me, 0, keepdims=False)
    gains = norm_gain[0]
    scales = time_scale[0]
    moments = timesteps(time_index[0, 0])
    cot_rows = cotangent_input[0, 0]
    normed_all = saved_normed[0, 0]
    inv_rows = saved_inv_rms[0, 0]
    saved_heads = saved_projections[0, 0, :, 0, :]
    rows = cot_rows.shape[0]
    owners = [jnp.bitwise_xor(me, mask) for mask in range(count)]

    cot_far = from_chips(cot_rows)
    moment = moments[0]
    hidden = layer_input[0, 0].astype(jnp.float32)
    tangent = tangent_input[0, 0].astype(jnp.float32)
    inverse = lax.rsqrt(jnp.mean(hidden * hidden, -1, keepdims=True) + EPS)
    normal = hidden * inverse
    tan_inverse = -(inverse**3) * jnp.mean(hidden * tangent, -1, keepdims=True)
    tan_normal = tangent * inverse + hidden * tan_inverse
    modulated = gains + jnp.sin(moment) * scales
    tan_modulated = jnp.cos(moment) * scales
    normed = (normal * modulated).astype(jnp.bfloat16)
    tan_normed = (tan_normal * modulated + normal * tan_modulated).astype(jnp.bfloat16)
    normed, tan_normed, cot_far = lax.optimization_barrier((normed, tan_normed, cot_far))
    cot_pieces = gathered(cot_rows, cot_far)
    normed_far = from_chips(normed)

    grad_out = jnp.zeros((rows * count, head_size), jnp.bfloat16)
    for mask in range(count):
        piece = jnp.einsum(
            "td,hd->th", cot_pieces[mask], output_head, preferred_element_type=jnp.float32
        ).astype(jnp.bfloat16)
        grad_out = lax.dynamic_update_slice_in_dim(grad_out, piece, owners[mask] * rows, 0)
    grad_q, grad_k, grad_v, attended_b = attend_backward(
        saved_heads[:, :head_size],
        saved_heads[:, head_size : 2 * head_size],
        saved_heads[:, 2 * head_size :],
        grad_out,
    )
    grad_proj = jnp.concatenate([grad_q, grad_k, grad_v], -1).astype(jnp.bfloat16)
    tan_normed, normed_far, grad_proj, attended_b = lax.optimization_barrier(
        (tan_normed, normed_far, grad_proj, attended_b)
    )
    tan_far = from_chips(tan_normed)
    normed_pieces = gathered(normed, normed_far)
    terms = {}
    for mask in reversed(range(count)):
        piece = lax.dynamic_slice_in_dim(grad_proj, owners[mask] * rows, rows, 0)
        terms[mask] = jnp.einsum(
            "tc,dc->td", piece, weight_heads, preferred_element_type=jnp.float32
        ).astype(jnp.bfloat16)
    grad_normed = summed_to_owner([terms[mask] for mask in range(count)])
    qkv_grad = jnp.einsum("td,tc->dc", normed_all, grad_proj, preferred_element_type=jnp.float32)
    out_grad = jnp.zeros((head_size, width), jnp.float32)
    for mask in range(count):
        piece = lax.dynamic_slice_in_dim(attended_b, owners[mask] * rows, rows, 0)
        out_grad = out_grad + jnp.einsum(
            "th,td->hd", piece, cot_pieces[mask], preferred_element_type=jnp.float32
        )
    qkv_total = scattered_over_dp(qkv_grad, 0)
    out_total = scattered_over_dp(out_grad, 1)

    def projected(pieces):
        return jnp.concatenate(
            [
                jnp.dot(piece, weight_heads, preferred_element_type=jnp.float32).astype(
                    jnp.bfloat16
                )
                for piece in pieces
            ]
        )

    proj = projected(normed_pieces)
    tan_proj = projected(gathered(tan_normed, tan_far))
    attended, tan_attended = attend_tangent(
        proj[:, :head_size],
        proj[:, head_size : 2 * head_size],
        proj[:, 2 * head_size :],
        tan_proj[:, :head_size],
        tan_proj[:, head_size : 2 * head_size],
        tan_proj[:, 2 * head_size :],
    )
    def to_rows(value):
        moved = jnp.zeros((rows, heads * head_size), jnp.bfloat16)
        for mask in range(count):
            piece = value[mask * rows : (mask + 1) * rows]
            if mask:
                piece = swapped(piece, "seq", mask)
            moved = lax.dynamic_update_slice_in_dim(moved, piece, owners[mask] * head_size, 1)
        return jnp.dot(moved, output_flat, preferred_element_type=jnp.float32)

    result = (hidden + to_rows(attended)).astype(jnp.bfloat16)
    next_input = passed_along(result, "section", 1)
    tan_result = (tangent + to_rows(tan_attended)).astype(jnp.bfloat16)
    tan_result, grad_late = lax.optimization_barrier((tan_result, grad_normed))
    next_tangent = passed_along(tan_result, "section", 1)

    moment = moments[1]
    own_normed = lax.dynamic_slice_in_dim(normed_all, me * rows, rows, 0)
    modulated = gains + jnp.sin(moment) * scales
    normal_b = own_normed.astype(jnp.float32) / modulated
    weighted = grad_normed * modulated
    grad_hidden = inv_rows[:, None] * (
        weighted - normal_b * jnp.mean(normal_b * weighted, -1, keepdims=True)
    )
    cotangent = (cot_rows.astype(jnp.float32) + grad_hidden).astype(jnp.bfloat16)
    cot_prev = passed_along(cotangent, "section", -1)
    gain_part = jnp.sum(grad_late * normal_b, 0)
    norm_total = summed_everywhere(jnp.stack([gain_part, jnp.sin(moment) * gain_part]))
    return (
        next_input[None, None],
        next_tangent[None, None],
        cot_prev[None, None],
        qkv_total[None, :, None, :],
        out_total[None, None],
        norm_total[None],
    )


def solution(mesh):
    placed = (
        P("section", "dp", "seq", None),
        P("section", "dp", "seq", None),
        P("section", "dp", "seq", None),
        P("section", "dp", None, None),
        P("section", "dp", "seq"),
        P("section", "dp", None, "seq", None),
        P("section", "dp", None),
        P("section", None, "seq", None),
        P("section", None, None, None),
        P("section", None),
        P("section", None),
    )
    return jax.shard_map(
        local,
        mesh=mesh,
        in_specs=placed,
        out_specs=(
            P("section", "dp", "seq", None),
            P("section", "dp", "seq", None),
            P("section", "dp", "seq", None),
            P("section", "dp", "seq", None),
            P("section", "seq", None, "dp"),
            P("section", None, None),
        ),
        check_vma=False,
    )
```

```python
import math

import jax
import jax.numpy as jnp
from jax import lax
from jax.sharding import PartitionSpec as P

TSTEPS = 1000


EPS = 1e-06


def passed_along(value, axis, steps):
    count = lax.axis_size(axis)
    pairs = [(source, (source + steps) % count) for source in range(count)]
    return lax.ppermute(value, axis, pairs)


def timesteps(indices):
    return math.pi / 2 * (indices.astype(jnp.float32) + 0.5) / TSTEPS


def attend(queries, keys, values):
    rows, head_size = queries.shape
    block_rows = min(512, rows)
    scale = 1.0 / math.sqrt(head_size)

    def one_block(query_block):
        scores = (
            jnp.einsum("qd,kd->qk", query_block, keys, preferred_element_type=jnp.float32) * scale
        )
        largest = jnp.max(scores, -1, keepdims=True)
        raised = jnp.exp(scores - largest)
        total = jnp.sum(raised, -1, keepdims=True)
        probs_low = (raised / total).astype(jnp.bfloat16)
        attended = jnp.dot(probs_low, values, preferred_element_type=jnp.float32)
        return (attended.astype(jnp.bfloat16), (largest, total))

    attended, kept = lax.map(one_block, queries.reshape(rows // block_rows, block_rows, -1))
    return (attended.reshape(rows, -1), kept)


def attend_tangent(kept, queries, keys, values, tan_queries, tan_keys, tan_values):
    rows, head_size = queries.shape
    block_rows = min(512, rows)
    scale = 1.0 / math.sqrt(head_size)

    def one_block(inputs):
        (largest, total), query_block, tangent_block = inputs
        scores = (
            jnp.einsum("qd,kd->qk", query_block, keys, preferred_element_type=jnp.float32) * scale
        )
        probs = jnp.exp(scores - largest) / total
        tan_scores = (
            jnp.einsum("qd,kd->qk", tangent_block, keys, preferred_element_type=jnp.float32)
            + jnp.einsum("qd,kd->qk", query_block, tan_keys, preferred_element_type=jnp.float32)
        ) * scale
        tan_probs = probs * (tan_scores - jnp.sum(probs * tan_scores, -1, keepdims=True))
        tan_attended = jnp.dot(
            tan_probs.astype(jnp.bfloat16), values, preferred_element_type=jnp.float32
        ) + jnp.dot(probs.astype(jnp.bfloat16), tan_values, preferred_element_type=jnp.float32)
        return tan_attended.astype(jnp.bfloat16)

    shaped = (
        kept,
        queries.reshape(rows // block_rows, block_rows, -1),
        tan_queries.reshape(rows // block_rows, block_rows, -1),
    )
    return lax.map(one_block, shaped).reshape(rows, -1)


def attend_backward(queries, keys, values, grad_attended):
    rows, head_size = queries.shape
    block_rows = min(512, rows)
    scale = 1.0 / math.sqrt(head_size)

    def one_block(carry, inputs):
        grad_keys, grad_values = carry
        query_block, grad_block = inputs
        scores = (
            jnp.einsum("qd,kd->qk", query_block, keys, preferred_element_type=jnp.float32) * scale
        )
        probs = jax.nn.softmax(scores, axis=-1)
        probs_low = probs.astype(jnp.bfloat16)
        attended = jnp.dot(probs_low, values, preferred_element_type=jnp.float32).astype(
            jnp.bfloat16
        )
        grad_values = grad_values + jnp.einsum(
            "qk,qd->kd", probs_low, grad_block, preferred_element_type=jnp.float32
        )
        grad_probs = jnp.einsum("qd,kd->qk", grad_block, values, preferred_element_type=jnp.float32)
        grad_scores = probs * (grad_probs - jnp.sum(probs * grad_probs, -1, keepdims=True)) * scale
        grad_low = grad_scores.astype(jnp.bfloat16)
        grad_queries = jnp.dot(grad_low, keys, preferred_element_type=jnp.float32)
        grad_keys = grad_keys + jnp.einsum(
            "qk,qd->kd", grad_low, query_block, preferred_element_type=jnp.float32
        )
        return ((grad_keys, grad_values), (grad_queries, attended))

    zeros = jnp.zeros((rows, head_size), jnp.float32)
    shaped = (
        queries.reshape(rows // block_rows, block_rows, head_size),
        grad_attended.reshape(rows // block_rows, block_rows, head_size),
    )
    (grad_keys, grad_values), (grad_queries, attended) = lax.scan(one_block, (zeros, zeros), shaped)
    return (
        grad_queries.reshape(rows, head_size),
        grad_keys,
        grad_values,
        attended.reshape(rows, head_size),
    )


def swapped(value, axis, mask):
    count = lax.axis_size(axis)
    return lax.ppermute(value, axis, [(source, source ^ mask) for source in range(count)])


def from_chips(value):
    return [swapped(value, "seq", mask) for mask in range(2, lax.axis_size("seq"), 2)]


def gathered(value, others):
    pieces = []
    for piece in [value] + others:
        pieces += [piece, swapped(piece, "seq", 1)]
    return pieces


def summed_on_chip(terms):
    pairs = []
    for mask in range(0, len(terms), 2):
        other = swapped(terms[mask ^ 1], "seq", 1)
        pair = terms[mask].astype(jnp.float32) + other.astype(jnp.float32)
        pairs.append(pair.astype(jnp.bfloat16) if mask else pair)
    return pairs


def scattered_over_dp(value, axis):
    count = lax.axis_size("dp")
    me = lax.axis_index("dp")
    length = value.shape[axis] // count
    total = lax.dynamic_slice_in_dim(value, me * length, length, axis)
    for step in range(1, count):
        part = lax.dynamic_slice_in_dim(value, lax.rem(me + step, count) * length, length, axis)
        total = total + passed_along(part.astype(jnp.bfloat16), "dp", step).astype(jnp.float32)
    return total


def summed_everywhere(value):
    for axis in ("seq", "dp"):
        mask = 1
        while mask < lax.axis_size(axis):
            value = value + swapped(value, axis, mask)
            mask *= 2
    return value


def local(
    layer_input,
    tangent_input,
    cotangent_input,
    saved_normed,
    saved_inv_rms,
    saved_projections,
    time_index,
    input_weight,
    output_weight,
    norm_gain,
    time_scale,
):
    count = lax.axis_size("seq")
    me = lax.axis_index("seq")
    weight_heads = input_weight[0, :, 0, :]
    output_whole = output_weight[0]
    heads, head_size, width = output_whole.shape
    output_flat = output_whole.reshape(heads * head_size, width)
    output_head = lax.dynamic_index_in_dim(output_whole, me, 0, keepdims=False)
    gains = norm_gain[0]
    scales = time_scale[0]
    moments = timesteps(time_index[0, 0])
    cot_rows = cotangent_input[0, 0]
    normed_all = saved_normed[0, 0]
    inv_rows = saved_inv_rms[0, 0]
    saved_heads = saved_projections[0, 0, :, 0, :]
    rows = cot_rows.shape[0]
    owners = [jnp.bitwise_xor(me, mask) for mask in range(count)]

    def in_pieces(value):
        return jnp.concatenate(
            [lax.dynamic_slice_in_dim(value, owner * rows, rows, 0) for owner in owners]
        )

    saved_heads = in_pieces(saved_heads)
    cot_far = from_chips(cot_rows)
    moment = moments[0]
    hidden = layer_input[0, 0].astype(jnp.float32)
    tangent = tangent_input[0, 0].astype(jnp.float32)
    inverse = lax.rsqrt(jnp.mean(hidden * hidden, -1, keepdims=True) + EPS)
    normal = hidden * inverse
    tan_inverse = -(inverse**3) * jnp.mean(hidden * tangent, -1, keepdims=True)
    tan_normal = tangent * inverse + hidden * tan_inverse
    modulated = gains + jnp.sin(moment) * scales
    tan_modulated = jnp.cos(moment) * scales
    normed = (normal * modulated).astype(jnp.bfloat16)
    tan_normed = (tan_normal * modulated + normal * tan_modulated).astype(jnp.bfloat16)
    normed, tan_normed, cot_far = lax.optimization_barrier((normed, tan_normed, cot_far))
    cot_pieces = gathered(cot_rows, cot_far)
    normed_far = from_chips(normed)

    grad_out = jnp.concatenate(
        [
            jnp.einsum(
                "td,hd->th", piece, output_head, preferred_element_type=jnp.float32
            ).astype(jnp.bfloat16)
            for piece in cot_pieces
        ]
    )
    grad_q, grad_k, grad_v, attended_b = attend_backward(
        saved_heads[:, :head_size],
        saved_heads[:, head_size : 2 * head_size],
        saved_heads[:, 2 * head_size :],
        grad_out,
    )
    grad_proj = jnp.concatenate([grad_q, grad_k, grad_v], -1).astype(jnp.bfloat16)
    terms = [
        jnp.einsum(
            "tc,dc->td",
            grad_proj[mask * rows : (mask + 1) * rows],
            weight_heads,
            preferred_element_type=jnp.float32,
        ).astype(jnp.bfloat16)
        for mask in range(count)
    ]
    pairs, grad_proj, attended_b = lax.optimization_barrier(
        (summed_on_chip(terms), grad_proj, attended_b)
    )
    grad_normed = pairs[0]
    for mask, pair in zip(range(2, count, 2), pairs[1:]):
        grad_normed = grad_normed + swapped(pair, "seq", mask).astype(jnp.float32)
    grad_proj = in_pieces(grad_proj)
    qkv_grad = jnp.einsum("td,tc->dc", normed_all, grad_proj, preferred_element_type=jnp.float32)
    out_grad = jnp.zeros((head_size, width), jnp.float32)
    for mask in range(count):
        piece = attended_b[mask * rows : (mask + 1) * rows]
        out_grad = out_grad + jnp.einsum(
            "th,td->hd", piece, cot_pieces[mask], preferred_element_type=jnp.float32
        )
    qkv_total = scattered_over_dp(qkv_grad, 0)
    out_total = scattered_over_dp(out_grad, 1)

    def projected(pieces):
        return jnp.concatenate(
            [
                jnp.dot(piece, weight_heads, preferred_element_type=jnp.float32).astype(
                    jnp.bfloat16
                )
                for piece in pieces
            ]
        )

    proj = projected(gathered(normed, normed_far))
    queries, keys, values = (
        proj[:, :head_size],
        proj[:, head_size : 2 * head_size],
        proj[:, 2 * head_size :],
    )

    def returned(value):
        pieces = [value[mask * rows : (mask + 1) * rows] for mask in range(count)]
        return pieces[:1] + [swapped(pieces[mask], "seq", mask) for mask in range(1, count)]

    def to_rows(pieces):
        moved = jnp.zeros((rows, heads * head_size), jnp.bfloat16)
        for owner, piece in zip(owners, pieces):
            moved = lax.dynamic_update_slice_in_dim(moved, piece, owner * head_size, 1)
        return jnp.dot(moved, output_flat, preferred_element_type=jnp.float32)

    attended, kept = attend(queries, keys, values)
    back = returned(attended)
    back, tan_normed = lax.optimization_barrier((back, tan_normed))
    tan_far = from_chips(tan_normed)
    result = (hidden + to_rows(back)).astype(jnp.bfloat16)
    next_input = passed_along(result, "section", 1)

    tan_proj = projected(gathered(tan_normed, tan_far))
    tan_attended = attend_tangent(
        kept,
        queries,
        keys,
        values,
        tan_proj[:, :head_size],
        tan_proj[:, head_size : 2 * head_size],
        tan_proj[:, 2 * head_size :],
    )
    tan_result = (tangent + to_rows(returned(tan_attended))).astype(jnp.bfloat16)
    moment = moments[1]
    own_normed = lax.dynamic_slice_in_dim(normed_all, me * rows, rows, 0)
    modulated = gains + jnp.sin(moment) * scales
    normal_b = own_normed.astype(jnp.float32) / modulated
    weighted = grad_normed * modulated
    grad_hidden = inv_rows[:, None] * (
        weighted - normal_b * jnp.mean(normal_b * weighted, -1, keepdims=True)
    )
    cotangent = (cot_rows.astype(jnp.float32) + grad_hidden).astype(jnp.bfloat16)
    cot_prev = passed_along(cotangent, "section", -1)
    tan_result, cot_prev = lax.optimization_barrier((tan_result, cot_prev))
    next_tangent = passed_along(tan_result, "section", 1)
    gain_part = jnp.sum(grad_normed * normal_b, 0)
    norm_total = summed_everywhere(jnp.stack([gain_part, jnp.sin(moment) * gain_part]))
    return (
        next_input[None, None],
        next_tangent[None, None],
        cot_prev[None, None],
        qkv_total[None, :, None, :],
        out_total[None, None],
        norm_total[None],
    )


def solution(mesh):
    placed = (
        P("section", "dp", "seq", None),
        P("section", "dp", "seq", None),
        P("section", "dp", "seq", None),
        P("section", "dp", None, None),
        P("section", "dp", "seq"),
        P("section", "dp", None, "seq", None),
        P("section", "dp", None),
        P("section", None, "seq", None),
        P("section", None, None, None),
        P("section", None),
        P("section", None),
    )
    return jax.shard_map(
        local,
        mesh=mesh,
        in_specs=placed,
        out_specs=(
            P("section", "dp", "seq", None),
            P("section", "dp", "seq", None),
            P("section", "dp", "seq", None),
            P("section", "dp", "seq", None),
            P("section", "seq", None, "dp"),
            P("section", None, None),
        ),
        check_vma=False,
    )
```

```python
import math

import jax
import jax.numpy as jnp
from jax import lax
from jax.sharding import PartitionSpec as P

TSTEPS = 1000


EPS = 1e-06


def passed_along(value, axis, steps):
    count = lax.axis_size(axis)
    pairs = [(source, (source + steps) % count) for source in range(count)]
    return lax.ppermute(value, axis, pairs)


def timesteps(indices):
    return math.pi / 2 * (indices.astype(jnp.float32) + 0.5) / TSTEPS


def attend(queries, keys, values):
    rows, head_size = queries.shape
    block_rows = min(512, rows)
    scale = 1.0 / math.sqrt(head_size)

    def one_block(query_block):
        scores = (
            jnp.einsum("qd,kd->qk", query_block, keys, preferred_element_type=jnp.float32) * scale
        )
        largest = jnp.max(scores, -1, keepdims=True)
        raised = jnp.exp(scores - largest)
        total = jnp.sum(raised, -1, keepdims=True)
        probs_low = (raised / total).astype(jnp.bfloat16)
        attended = jnp.dot(probs_low, values, preferred_element_type=jnp.float32)
        return (attended.astype(jnp.bfloat16), (largest, total))

    attended, kept = lax.map(one_block, queries.reshape(rows // block_rows, block_rows, -1))
    return (attended.reshape(rows, -1), kept)


def attend_tangent(kept, queries, keys, values, tan_queries, tan_keys, tan_values):
    rows, head_size = queries.shape
    block_rows = min(512, rows)
    scale = 1.0 / math.sqrt(head_size)

    def one_block(inputs):
        (largest, total), query_block, tangent_block = inputs
        scores = (
            jnp.einsum("qd,kd->qk", query_block, keys, preferred_element_type=jnp.float32) * scale
        )
        probs = jnp.exp(scores - largest) / total
        tan_scores = (
            jnp.einsum("qd,kd->qk", tangent_block, keys, preferred_element_type=jnp.float32)
            + jnp.einsum("qd,kd->qk", query_block, tan_keys, preferred_element_type=jnp.float32)
        ) * scale
        tan_probs = probs * (tan_scores - jnp.sum(probs * tan_scores, -1, keepdims=True))
        tan_attended = jnp.dot(
            tan_probs.astype(jnp.bfloat16), values, preferred_element_type=jnp.float32
        ) + jnp.dot(probs.astype(jnp.bfloat16), tan_values, preferred_element_type=jnp.float32)
        return tan_attended.astype(jnp.bfloat16)

    shaped = (
        kept,
        queries.reshape(rows // block_rows, block_rows, -1),
        tan_queries.reshape(rows // block_rows, block_rows, -1),
    )
    return lax.map(one_block, shaped).reshape(rows, -1)


def attend_backward(queries, keys, values, grad_attended):
    rows, head_size = queries.shape
    block_rows = min(512, rows)
    scale = 1.0 / math.sqrt(head_size)

    def one_block(carry, inputs):
        grad_keys, grad_values = carry
        query_block, grad_block = inputs
        scores = (
            jnp.einsum("qd,kd->qk", query_block, keys, preferred_element_type=jnp.float32) * scale
        )
        probs = jax.nn.softmax(scores, axis=-1)
        probs_low = probs.astype(jnp.bfloat16)
        attended = jnp.dot(probs_low, values, preferred_element_type=jnp.float32).astype(
            jnp.bfloat16
        )
        grad_values = grad_values + jnp.einsum(
            "qk,qd->kd", probs_low, grad_block, preferred_element_type=jnp.float32
        )
        grad_probs = jnp.einsum("qd,kd->qk", grad_block, values, preferred_element_type=jnp.float32)
        grad_scores = probs * (grad_probs - jnp.sum(probs * grad_probs, -1, keepdims=True)) * scale
        grad_low = grad_scores.astype(jnp.bfloat16)
        grad_queries = jnp.dot(grad_low, keys, preferred_element_type=jnp.float32)
        grad_keys = grad_keys + jnp.einsum(
            "qk,qd->kd", grad_low, query_block, preferred_element_type=jnp.float32
        )
        return ((grad_keys, grad_values), (grad_queries, attended))

    zeros = jnp.zeros((rows, head_size), jnp.float32)
    shaped = (
        queries.reshape(rows // block_rows, block_rows, head_size),
        grad_attended.reshape(rows // block_rows, block_rows, head_size),
    )
    (grad_keys, grad_values), (grad_queries, attended) = lax.scan(one_block, (zeros, zeros), shaped)
    return (
        grad_queries.reshape(rows, head_size),
        grad_keys,
        grad_values,
        attended.reshape(rows, head_size),
    )


def swapped(value, axis, mask):
    count = lax.axis_size(axis)
    return lax.ppermute(value, axis, [(source, source ^ mask) for source in range(count)])


def from_chips(value):
    return [swapped(value, "seq", mask) for mask in range(2, lax.axis_size("seq"), 2)]


def gathered(value, others):
    pieces = []
    for piece in [value] + others:
        pieces += [piece, swapped(piece, "seq", 1)]
    return pieces


def summed_on_chip(terms):
    pairs = []
    for mask in range(0, len(terms), 2):
        other = swapped(terms[mask ^ 1], "seq", 1)
        pair = terms[mask].astype(jnp.float32) + other.astype(jnp.float32)
        pairs.append(pair.astype(jnp.bfloat16) if mask else pair)
    return pairs


def scattered_over_dp(value, axis):
    count = lax.axis_size("dp")
    me = lax.axis_index("dp")
    length = value.shape[axis] // count
    total = lax.dynamic_slice_in_dim(value, me * length, length, axis)
    for step in range(1, count):
        part = lax.dynamic_slice_in_dim(value, lax.rem(me + step, count) * length, length, axis)
        total = total + passed_along(part.astype(jnp.bfloat16), "dp", step).astype(jnp.float32)
    return total


def summed_everywhere(value):
    for axis in ("seq", "dp"):
        mask = 1
        while mask < lax.axis_size(axis):
            value = value + swapped(value, axis, mask)
            mask *= 2
    return value


def local(
    layer_input,
    tangent_input,
    cotangent_input,
    saved_normed,
    saved_inv_rms,
    saved_projections,
    time_index,
    input_weight,
    output_weight,
    norm_gain,
    time_scale,
):
    count = lax.axis_size("seq")
    me = lax.axis_index("seq")
    weight_heads = input_weight[0, :, 0, :]
    output_whole = output_weight[0]
    heads, head_size, width = output_whole.shape
    output_flat = output_whole.reshape(heads * head_size, width)
    output_head = lax.dynamic_index_in_dim(output_whole, me, 0, keepdims=False)
    gains = norm_gain[0]
    scales = time_scale[0]
    moments = timesteps(time_index[0, 0])
    cot_rows = cotangent_input[0, 0]
    normed_all = saved_normed[0, 0]
    inv_rows = saved_inv_rms[0, 0]
    saved_heads = saved_projections[0, 0, :, 0, :]
    rows = cot_rows.shape[0]
    owners = [jnp.bitwise_xor(me, mask) for mask in range(count)]

    def in_pieces(value):
        return jnp.concatenate(
            [lax.dynamic_slice_in_dim(value, owner * rows, rows, 0) for owner in owners]
        )

    saved_heads = in_pieces(saved_heads)
    cot_far = from_chips(cot_rows)
    moment = moments[0]
    hidden = layer_input[0, 0].astype(jnp.float32)
    tangent = tangent_input[0, 0].astype(jnp.float32)
    inverse = lax.rsqrt(jnp.mean(hidden * hidden, -1, keepdims=True) + EPS)
    normal = hidden * inverse
    tan_inverse = -(inverse**3) * jnp.mean(hidden * tangent, -1, keepdims=True)
    tan_normal = tangent * inverse + hidden * tan_inverse
    modulated = gains + jnp.sin(moment) * scales
    tan_modulated = jnp.cos(moment) * scales
    normed = (normal * modulated).astype(jnp.bfloat16)
    tan_normed = (tan_normal * modulated + normal * tan_modulated).astype(jnp.bfloat16)
    normed, tan_normed, cot_far = lax.optimization_barrier((normed, tan_normed, cot_far))
    cot_pieces = gathered(cot_rows, cot_far)
    normed_far = from_chips(normed)

    grad_out = jnp.concatenate(
        [
            jnp.einsum(
                "td,hd->th", piece, output_head, preferred_element_type=jnp.float32
            ).astype(jnp.bfloat16)
            for piece in cot_pieces
        ]
    )
    grad_q, grad_k, grad_v, attended_b = attend_backward(
        saved_heads[:, :head_size],
        saved_heads[:, head_size : 2 * head_size],
        saved_heads[:, 2 * head_size :],
        grad_out,
    )
    grad_proj = jnp.concatenate([grad_q, grad_k, grad_v], -1).astype(jnp.bfloat16)
    terms = [
        jnp.einsum(
            "tc,dc->td",
            grad_proj[mask * rows : (mask + 1) * rows],
            weight_heads,
            preferred_element_type=jnp.float32,
        ).astype(jnp.bfloat16)
        for mask in range(count)
    ]
    terms, grad_proj, attended_b = lax.optimization_barrier((terms, grad_proj, attended_b))
    pairs, normed_far = lax.optimization_barrier((summed_on_chip(terms), normed_far))
    grad_normed = pairs[0]
    for mask, pair in zip(range(2, count, 2), pairs[1:]):
        grad_normed = grad_normed + swapped(pair, "seq", mask).astype(jnp.float32)
    grad_proj = in_pieces(grad_proj)
    qkv_grad = jnp.einsum("td,tc->dc", normed_all, grad_proj, preferred_element_type=jnp.float32)
    out_grad = jnp.zeros((head_size, width), jnp.float32)
    for mask in range(count):
        piece = attended_b[mask * rows : (mask + 1) * rows]
        out_grad = out_grad + jnp.einsum(
            "th,td->hd", piece, cot_pieces[mask], preferred_element_type=jnp.float32
        )
    qkv_total = scattered_over_dp(qkv_grad, 0)
    out_total = scattered_over_dp(out_grad, 1)

    def projected(pieces):
        return jnp.concatenate(
            [
                jnp.dot(piece, weight_heads, preferred_element_type=jnp.float32).astype(
                    jnp.bfloat16
                )
                for piece in pieces
            ]
        )

    proj = projected(gathered(normed, normed_far))
    queries, keys, values = (
        proj[:, :head_size],
        proj[:, head_size : 2 * head_size],
        proj[:, 2 * head_size :],
    )

    def returned(value):
        pieces = [value[mask * rows : (mask + 1) * rows] for mask in range(count)]
        return pieces[:1] + [swapped(pieces[mask], "seq", mask) for mask in range(1, count)]

    def to_rows(pieces):
        moved = jnp.zeros((rows, heads * head_size), jnp.bfloat16)
        for owner, piece in zip(owners, pieces):
            moved = lax.dynamic_update_slice_in_dim(moved, piece, owner * head_size, 1)
        return jnp.dot(moved, output_flat, preferred_element_type=jnp.float32)

    attended, kept = attend(queries, keys, values)
    back = returned(attended)
    back, grad_normed, tan_normed = lax.optimization_barrier((back, grad_normed, tan_normed))
    tan_far = from_chips(tan_normed)
    result = (hidden + to_rows(back)).astype(jnp.bfloat16)
    next_input = passed_along(result, "section", 1)

    tan_proj = projected(gathered(tan_normed, tan_far))
    tan_attended = attend_tangent(
        kept,
        queries,
        keys,
        values,
        tan_proj[:, :head_size],
        tan_proj[:, head_size : 2 * head_size],
        tan_proj[:, 2 * head_size :],
    )
    tan_result = (tangent + to_rows(returned(tan_attended))).astype(jnp.bfloat16)
    moment = moments[1]
    own_normed = lax.dynamic_slice_in_dim(normed_all, me * rows, rows, 0)
    modulated = gains + jnp.sin(moment) * scales
    normal_b = own_normed.astype(jnp.float32) / modulated
    weighted = grad_normed * modulated
    grad_hidden = inv_rows[:, None] * (
        weighted - normal_b * jnp.mean(normal_b * weighted, -1, keepdims=True)
    )
    cotangent = (cot_rows.astype(jnp.float32) + grad_hidden).astype(jnp.bfloat16)
    cot_prev = passed_along(cotangent, "section", -1)
    tan_result, cot_prev = lax.optimization_barrier((tan_result, cot_prev))
    next_tangent = passed_along(tan_result, "section", 1)
    gain_part = jnp.sum(grad_normed * normal_b, 0)
    norm_total = summed_everywhere(jnp.stack([gain_part, jnp.sin(moment) * gain_part]))
    return (
        next_input[None, None],
        next_tangent[None, None],
        cot_prev[None, None],
        qkv_total[None, :, None, :],
        out_total[None, None],
        norm_total[None],
    )


def solution(mesh):
    placed = (
        P("section", "dp", "seq", None),
        P("section", "dp", "seq", None),
        P("section", "dp", "seq", None),
        P("section", "dp", None, None),
        P("section", "dp", "seq"),
        P("section", "dp", None, "seq", None),
        P("section", "dp", None),
        P("section", None, "seq", None),
        P("section", None, None, None),
        P("section", None),
        P("section", None),
    )
    return jax.shard_map(
        local,
        mesh=mesh,
        in_specs=placed,
        out_specs=(
            P("section", "dp", "seq", None),
            P("section", "dp", "seq", None),
            P("section", "dp", "seq", None),
            P("section", "dp", "seq", None),
            P("section", "seq", None, "dp"),
            P("section", None, None),
        ),
        check_vma=False,
    )
```
